512 devices in a mesh: prompt: 16 (over z_lo, x, core), resp: 32 (over y, z_hi).
Axes of the slice: x: 4, y: 8, z: 8 (z_hi: 4, z_lo: 2; z = z_hi * 2 + z_lo), core: 2. Of those that a mesh axis runs over, the one named last changes fastest.
Arguments:
- prefix_input: bfloat16 [16, 2048, 5120], P('prompt', 'resp'), may hold values from -6 to 6
- prefix_query_rows: bfloat16 [16, 2048, 2560], P('prompt', 'resp'), may hold values from -10 to 10
- prefix_key_rows: bfloat16 [16, 2048, 512], P('prompt', 'resp'), may hold values from -2.5 to 2.5
- prefix_value_rows: bfloat16 [16, 2048, 512], P('prompt', 'resp'), may hold values from -6 to 6
- prefix_output: bfloat16 [16, 2048, 2560], P('prompt', 'resp'), may hold values from -3 to 3
- prefix_output_grad: bfloat16 [16, 2048, 2560], P('prompt', 'resp'), may hold values from -6 to 6
- prefix_middle: bfloat16 [16, 2048, 64], P('prompt', 'resp'), may hold values from -6 to 6
- response_input: bfloat16 [16, 32, 64, 5120], P('prompt', 'resp'), may hold values from -6 to 6
- response_query: bfloat16 [16, 32, 64, 2560], P('prompt', 'resp'), may hold values from -10 to 10
- response_key: bfloat16 [16, 32, 64, 512], P('prompt', 'resp'), may hold values from -2.5 to 2.5
- response_value: bfloat16 [16, 32, 64, 512], P('prompt', 'resp'), may hold values from -6 to 6
- response_output: bfloat16 [16, 32, 64, 2560], P('prompt', 'resp'), may hold values from -3 to 3
- response_output_grad: bfloat16 [16, 32, 64, 2560], P('prompt', 'resp'), may hold values from -6 to 6
- response_middle: bfloat16 [16, 32, 64, 64], P('prompt', 'resp'), may hold values from -6 to 6
- lengths: int32 [16, 32], P('prompt', 'resp'), may hold values from 1 to 64, 1024 in all within a row
- adapter_up_weight: bfloat16 [64, 2560], replicated, may hold values from -0.75 to 0.75
Outputs:
- prefix_dkey: bfloat16 [16, 2048, 512], P('prompt', 'resp')
- prefix_dvalue: bfloat16 [16, 2048, 512], P('prompt', 'resp')
- resp_dkey: bfloat16 [16, 32, 64, 512], P('prompt', 'resp')
- resp_dvalue: bfloat16 [16, 32, 64, 512], P('prompt', 'resp')
- down_weight_grad: float32 [5120, 64], replicated
- up_weight_grad: float32 [64, 2560], replicated
The draws below stay inside these ranges and needn't reach their ends.
Inputs may be any that keep to these rules, and one draw needn't show every extreme that they name: For each prompt the 32 lengths sum to 1024 and the longest is exactly 64.
All inputs are finite; a program needn't handle non-finite values. No bound on the sum of `lengths` on one device may be relied on, other than what follows from the above.
Results may differ from the reference program's by a relative error of at most 0.018.
Values may be sent and summed in bfloat16 or wider, within the bound.
A program may use at most 128 MiB of HBM per device.

```python
import math
import jax
import jax.numpy as jnp
import numpy as np
from jax import lax

D = 5120
HEAD_SIZE = 128
QUERY_HEAD_COUNT = 20
KVH = 4
ADAPTER_RANK = 64
RL = 64
PREF_DEV = 64
PREFIX = 2048
RESPS = 32
PROMPTS = 16
N_RESP = 32


def paired_fields(key, salt, query_shape, key_shape, edge, share):
    base = jax.random.fold_in(key, salt)
    raw_keys = jax.random.normal(jax.random.fold_in(base, 11), key_shape, jnp.float32)
    key_field = jnp.where(edge > 0.0, edge * jnp.sign(raw_keys), jnp.clip(raw_keys, -2.5, 2.5))
    row_count = key_shape[-2]
    odd_rows = jnp.arange(row_count) % 2 == 1
    chosen = jax.random.bernoulli(jax.random.fold_in(base, 12), share, key_shape[:-1]) & odd_rows
    strength = 2.0 + jax.random.randint(jax.random.fold_in(base, 13), key_shape[:-1], 0, 3).astype(jnp.float32)
    heads_four = key_field.reshape(key_shape[:-1] + (KVH, HEAD_SIZE))
    spread = jnp.repeat(heads_four, QUERY_HEAD_COUNT // KVH, axis=-2).reshape(query_shape)
    raw_query = jnp.clip(jax.random.normal(jax.random.fold_in(base, 14), query_shape, jnp.float32), -4.0, 4.0)
    query_field = jnp.where(chosen[..., None], strength[..., None] * spread, raw_query)
    following = jnp.roll(heads_four, -1, axis=-3)
    first_col = jnp.arange(HEAD_SIZE) == 0
    following = jnp.where(first_col, 0.0, following).reshape(key_shape)
    marked = jnp.roll(chosen, -1, axis=-1)
    key_field = jnp.where(marked[..., None], following, key_field)
    return (query_field, key_field)


def prefix_pair(key):
    return paired_fields(key, 100, (PROMPTS, PREFIX, QUERY_HEAD_COUNT * HEAD_SIZE), (PROMPTS, PREFIX, KVH * HEAD_SIZE), 0.0, 0.0)


def resp_pair(key):
    return paired_fields(key, 200, (PROMPTS, RESPS, RL, QUERY_HEAD_COUNT * HEAD_SIZE), (PROMPTS, RESPS, RL, KVH * HEAD_SIZE), 0.0, 0.0)


def draw_prefix_query_rows(key, part):
    return prefix_pair(key)[0].astype(jnp.bfloat16)


def draw_prefix_key_rows(key, part):
    return prefix_pair(key)[1].astype(jnp.bfloat16)


def draw_response_query(key, part):
    return resp_pair(key)[0].astype(jnp.bfloat16)


def draw_response_key(key, part):
    return resp_pair(key)[1].astype(jnp.bfloat16)


def block_levels(stream_key, dims, cuts, smallest, high):
    factor_of = 1.0
    for axis_at, parts in cuts:
        steps = jax.random.uniform(jax.random.fold_in(jax.random.fold_in(stream_key, 6), axis_at), (parts,), jnp.float32, smallest / len(cuts), high / len(cuts))
        factor_of = factor_of * jnp.repeat(jnp.exp(steps), dims[axis_at] // parts).reshape((-1,) + (1,) * (len(dims) - 1 - axis_at))
    return factor_of


def length_profile(number_of, total, bound, skew):
    weights = [(1 << 20) // math.isqrt(rank ** skew) + 1 for rank in range(2, number_of + 1)]
    rest, given = total - bound - (number_of - 1), [1] * (number_of - 1)
    while rest > 0:
        candidates = [i for i in range(number_of - 1) if given[i] < bound]
        mass, left = sum([weights[i] for i in candidates]), rest
        for i in candidates:
            more = min(bound - given[i], max(1, left * weights[i] // mass), rest)
            given[i] = given[i] + more
            rest = rest - more
    return np.array([bound] + given)


def uneven(own_key, number_of, total, reach, slope):
    if number_of == 2:
        one = jax.random.randint(own_key, (), max(1, total - reach), min(reach, total - 1) + 1)
        return jnp.stack([one, total - one])
    sizes = jnp.asarray(length_profile(number_of, total, reach, slope), jnp.int32)
    twos = (number_of - 1) // 2
    donor, receiver = sizes[1:1 + 2 * twos:2], sizes[2:2 + 2 * twos:2]
    margin = jnp.minimum(donor - 1, reach - receiver)
    moved = jax.random.randint(jax.random.fold_in(own_key, 1), (twos,), 0, 1 << 20) % (margin + 1)
    sizes = sizes.at[1:1 + 2 * twos:2].set(donor - moved).at[2:2 + 2 * twos:2].set(receiver + moved)
    return sizes[jax.random.permutation(jax.random.fold_in(own_key, 2), number_of)]


def bell_draw(key, extent, scale, reach, pieces=(), kind=jnp.bfloat16):
    values = scale * jax.random.normal(key, extent, jnp.float32)
    if pieces:
        values = values * block_levels(key, extent, pieces, -0.22, 0.18)
    return jnp.clip(values, -reach, reach).astype(kind)


def setup_inputs(seed: int = 0) -> dict:
    seeds = jax.random.split(jax.random.key(seed), 17)
    prefix_input = bell_draw(seeds[0], (PROMPTS, PREFIX, D), 1.0, 6.0, ((0, 16), (1, 32)))
    prefix_query_rows = draw_prefix_query_rows(jax.random.fold_in(seeds[16], 71), 0)
    prefix_key_rows = draw_prefix_key_rows(jax.random.fold_in(seeds[16], 71), 0)
    prefix_value_rows = bell_draw(seeds[3], (PROMPTS, PREFIX, KVH * HEAD_SIZE), 1.0, 6.0, ((0, 16), (1, 32)))
    prefix_output = bell_draw(seeds[4], (PROMPTS, PREFIX, QUERY_HEAD_COUNT * HEAD_SIZE), 0.5, 3.0, ((0, 16), (1, 32)))
    prefix_output_grad = bell_draw(seeds[5], (PROMPTS, PREFIX, QUERY_HEAD_COUNT * HEAD_SIZE), 1.0, 6.0, ((0, 16), (1, 32)))
    prefix_middle = bell_draw(seeds[6], (PROMPTS, PREFIX, ADAPTER_RANK), 1.0, 6.0, ((0, 16), (1, 32)))
    response_input = bell_draw(seeds[7], (PROMPTS, RESPS, RL, D), 1.0, 6.0, ((0, 16), (1, 32)))
    response_query = draw_response_query(jax.random.fold_in(seeds[16], 71), 0)
    response_key = draw_response_key(jax.random.fold_in(seeds[16], 71), 0)
    response_value = bell_draw(seeds[10], (PROMPTS, RESPS, RL, KVH * HEAD_SIZE), 1.0, 6.0, ((0, 16), (1, 32)))
    response_output = bell_draw(seeds[11], (PROMPTS, RESPS, RL, QUERY_HEAD_COUNT * HEAD_SIZE), 0.5, 3.0, ((0, 16), (1, 32)))
    response_output_grad = bell_draw(seeds[12], (PROMPTS, RESPS, RL, QUERY_HEAD_COUNT * HEAD_SIZE), 1.0, 6.0, ((0, 16), (1, 32)))
    response_middle = bell_draw(seeds[13], (PROMPTS, RESPS, RL, ADAPTER_RANK), 1.0, 6.0, ((0, 16), (1, 32)))
    lengths = jax.vmap(lambda own: uneven(own, RESPS, RESPS * RL // 2, RL, 2))(jax.random.split(seeds[14], PROMPTS)).reshape((PROMPTS, RESPS)).astype(jnp.int32)
    adapter_up_weight = bell_draw(seeds[15], (ADAPTER_RANK, QUERY_HEAD_COUNT * HEAD_SIZE), ADAPTER_RANK ** -0.5, 0.75)
    return {"prefix_input": prefix_input, "prefix_query_rows": prefix_query_rows, "prefix_key_rows": prefix_key_rows, "prefix_value_rows": prefix_value_rows, "prefix_output": prefix_output, "prefix_output_grad": prefix_output_grad, "prefix_middle": prefix_middle, "response_input": response_input, "response_query": response_query, "response_key": response_key, "response_value": response_value, "response_output": response_output, "response_output_grad": response_output_grad, "response_middle": response_middle, "lengths": lengths, "adapter_up_weight": adapter_up_weight}


adapter_factor = 2.0


def attention_back(query_rows, key_rows, value_rows, grad_rows, out_rows, visible):
    total_rows = query_rows.shape[0]
    total_cols = key_rows.shape[0]
    groups = QUERY_HEAD_COUNT // KVH
    heads_q = query_rows.reshape(total_rows, KVH, groups, HEAD_SIZE).astype(jnp.float32)
    heads_k = key_rows.reshape(total_cols, KVH, HEAD_SIZE).astype(jnp.float32)
    heads_v = value_rows.reshape(total_cols, KVH, HEAD_SIZE).astype(jnp.float32)
    heads_o = grad_rows.reshape(total_rows, KVH, groups, HEAD_SIZE).astype(jnp.float32)
    heads_f = out_rows.reshape(total_rows, KVH, groups, HEAD_SIZE).astype(jnp.float32)
    scaling = HEAD_SIZE ** -0.5
    scores = scaling * jnp.einsum("rkgd,ckd->kgrc", heads_q, heads_k)
    scores = jnp.where(visible[None, None], scores, -jnp.inf)
    maxima = jnp.max(scores, axis=-1, keepdims=True)
    exp_terms = jnp.exp(scores - maxima)
    probs_full = exp_terms / jnp.sum(exp_terms, axis=-1, keepdims=True)
    probs_low = lax.optimization_barrier(probs_full.astype(jnp.bfloat16)).astype(jnp.float32)
    row_delta = jnp.sum(heads_o * heads_f, axis=-1)
    grad_probs = jnp.einsum("rkgd,ckd->kgrc", heads_o, heads_v)
    grad_scores = probs_full * (grad_probs - jnp.transpose(row_delta, (1, 2, 0))[..., None])
    scores_low = lax.optimization_barrier(grad_scores.astype(jnp.bfloat16)).astype(jnp.float32)
    query_gradient = scaling * jnp.einsum("kgrc,ckd->rkgd", scores_low, heads_k)
    grad_key = scaling * jnp.einsum("kgrc,rkgd->ckd", scores_low, heads_q)
    grad_value = jnp.einsum("kgrc,rkgd->ckd", probs_low, heads_o)
    return (query_gradient.reshape(total_rows, QUERY_HEAD_COUNT * HEAD_SIZE), grad_key.reshape(total_cols, KVH * HEAD_SIZE),
            grad_value.reshape(total_cols, KVH * HEAD_SIZE))


def adapter_pieces(input_arrays, middle_rows, query_gradient, adapter_up_weight):
    query_reduced = query_gradient.astype(jnp.bfloat16)
    up_piece = jnp.dot(middle_rows.T, query_reduced, preferred_element_type=jnp.float32)
    hidden_reduced = jnp.dot(query_reduced, adapter_up_weight.T, preferred_element_type=jnp.float32).astype(jnp.bfloat16)
    down_piece = jnp.dot(input_arrays.T, hidden_reduced, preferred_element_type=jnp.float32)
    return down_piece, up_piece


def rounded(values):
    return lax.optimization_barrier(values.astype(jnp.bfloat16)).astype(jnp.float32)


def reference(prefix_input, prefix_query_rows, prefix_key_rows, prefix_value_rows, prefix_output, prefix_output_grad, prefix_middle,
              response_input, response_query, response_key, response_value, response_output, response_output_grad, response_middle, lengths, adapter_up_weight):
    rows_all = PREF_DEV + RL
    cols_all = PREFIX + RL
    row_index = jnp.arange(rows_all, dtype=jnp.int32)[:, None]
    col_index = jnp.arange(cols_all, dtype=jnp.int32)[None, :]
    prefix_col = col_index < PREFIX
    resp_visible = prefix_col | (col_index - PREFIX <= row_index - PREF_DEV)

    def blocks(array):
        return array.reshape((N_RESP, PREF_DEV) + array.shape[1:])

    def one_prompt(prompt_data):
        (pre_inputs, pre_query, pre_key, pre_value, pre_out, pre_grad, pre_mid,
         res_inputs, res_query, res_key, res_value, res_out, res_grad, res_mid, res_lengths) = prompt_data

        def one_block(carry, block):
            acc_key, acc_value, down_sum, up_sum = carry
            (block_index, b_inputs, b_query, b_out, b_grad, b_mid,
             one_inputs, one_query, one_key, one_value, one_out, one_grad, one_mid, one_length) = block
            alive_rows = jnp.arange(RL, dtype=jnp.int32) < one_length
            masked_grad = jnp.where(alive_rows[:, None], one_grad, jnp.zeros_like(one_grad))
            pre_visible = prefix_col & (col_index <= block_index * PREF_DEV + row_index)
            visible = jnp.where(row_index < PREF_DEV, pre_visible, resp_visible)
            query_rows = jnp.concatenate([b_query, one_query], axis=0)
            key_rows = jnp.concatenate([pre_key, one_key], axis=0)
            value_rows = jnp.concatenate([pre_value, one_value], axis=0)
            grad_rows = jnp.concatenate([b_grad, masked_grad], axis=0)
            out_rows = jnp.concatenate([b_out, one_out], axis=0)
            query_gradient, grad_key, grad_value = attention_back(query_rows, key_rows, value_rows, grad_rows,
                                                              out_rows, visible)
            input_arrays = jnp.concatenate([b_inputs, one_inputs], axis=0)
            middle_rows = jnp.concatenate([b_mid, one_mid], axis=0)
            down_piece, up_piece = adapter_pieces(input_arrays, middle_rows, query_gradient, adapter_up_weight)
            new_carry = (acc_key + rounded(grad_key[:PREFIX]), acc_value + rounded(grad_value[:PREFIX]),
                         down_sum + down_piece, up_sum + up_piece)
            return new_carry, (grad_key[PREFIX:].astype(jnp.bfloat16), grad_value[PREFIX:].astype(jnp.bfloat16))

        start_carry = (jnp.zeros((PREFIX, KVH * HEAD_SIZE), jnp.float32), jnp.zeros((PREFIX, KVH * HEAD_SIZE), jnp.float32),
                       jnp.zeros((D, ADAPTER_RANK), jnp.float32), jnp.zeros((ADAPTER_RANK, QUERY_HEAD_COUNT * HEAD_SIZE), jnp.float32))
        final_carry, resp_grads = lax.scan(one_block, start_carry,
                                           (jnp.arange(N_RESP, dtype=jnp.int32), blocks(pre_inputs),
                                            blocks(pre_query), blocks(pre_out), blocks(pre_grad), blocks(pre_mid),
                                            res_inputs, res_query, res_key, res_value, res_out, res_grad,
                                            res_mid, res_lengths))
        acc_key, acc_value, down_sum, up_sum = final_carry
        return (acc_key.astype(jnp.bfloat16), acc_value.astype(jnp.bfloat16),
                resp_grads[0], resp_grads[1], down_sum, up_sum)

    results = lax.map(one_prompt, (prefix_input, prefix_query_rows, prefix_key_rows, prefix_value_rows, prefix_output, prefix_output_grad,
                                   prefix_middle, response_input, response_query, response_key, response_value, response_output, response_output_grad,
                                   response_middle, lengths))
    prefix_dkey, prefix_dvalue, resp_dkey, resp_dvalue, down_grad_full, up_grad_full = results
    down_weight_grad = adapter_factor * jnp.sum(down_grad_full, axis=0)
    up_weight_grad = adapter_factor * jnp.sum(up_grad_full, axis=0)
    return prefix_dkey, prefix_dvalue, resp_dkey, resp_dvalue, down_weight_grad, up_weight_grad
```

```python
import functools
import math

import jax
import jax.numpy as jnp
from jax import lax
from jax.experimental import pallas as pl
from jax.experimental.pallas import tpu as pltpu
from jax.sharding import PartitionSpec as P

ZL, X, C, Y, ZH = 2, 4, 2, 8, 4
HD = 128
ROWS = 64
KVH = 4
GROUPS = 5
RANK = 64
LANES = 512
GROUP_LANES = GROUPS * HD
QL = 2 * ROWS * GROUPS
SCALE = HD ** -0.5
LOG2E = math.log2(math.e)
F32 = jnp.float32
BF16 = jnp.bfloat16
MESH = pl.DeviceIdType.MESH


def mod(a, n):
    return lax.rem(a + n, n)


def nt(a, b):
    return lax.dot_general(a, b, (((1,), (1,)), ((), ())), preferred_element_type=F32)


def nn(a, b):
    return lax.dot_general(a, b, (((1,), (0,)), ((), ())), preferred_element_type=F32)


def tn(a, b):
    return lax.dot_general(a, b, (((0,), (0,)), ((), ())), preferred_element_type=F32)


class Place:
    def __init__(self):
        p, r = lax.axis_index("prompt"), lax.axis_index("resp")
        self.p, self.r = p, r
        self.core = lax.rem(p, C)
        self.x = lax.rem(lax.div(p, C), X)
        self.zl = lax.div(p, C * X)
        self.y = lax.div(r, ZH)
        self.zh = lax.rem(r, ZH)
        self.z = self.zh * ZL + self.zl

    def device(self, core=None, x=None, y=None, z=None):
        core = self.core if core is None else core
        x = self.x if x is None else x
        y = self.y if y is None else y
        z = self.z if z is None else z
        zl, zh = lax.rem(z, ZL), lax.div(z, ZL)
        return {"prompt": (zl * X + x) * C + core, "resp": y * ZH + zh}


def entry_barrier(at):
    barrier = pltpu.get_barrier_semaphore()
    count = 0
    for off in range(1, C):
        pl.semaphore_signal(barrier, inc=1, device_id=at.device(core=mod(at.core + off, C)), device_id_type=MESH)
        count += 1
    for off in range(1, X):
        pl.semaphore_signal(barrier, inc=1, device_id=at.device(x=mod(at.x + off, X)), device_id_type=MESH)
        count += 1
    for off in range(1, Y):
        pl.semaphore_signal(barrier, inc=1, device_id=at.device(y=mod(at.y + off, Y)), device_id_type=MESH)
        count += 1
    for off in range(1, ZH * ZL):
        pl.semaphore_signal(barrier, inc=1, device_id=at.device(z=mod(at.z + off, ZH * ZL)), device_id_type=MESH)
        count += 1
    pl.semaphore_wait(barrier, count)


def rcopy(src, dst, send, recv, device):
    return pltpu.make_async_remote_copy(
        src_ref=src, dst_ref=dst, send_sem=send, recv_sem=recv, device_id=device, device_id_type=MESH)


def rows_at(start, count):
    return pl.ds(pl.multiple_of(start, ROWS), count)


def each(n, body):
    def step(i, carry):
        body(i)
        return carry
    lax.fori_loop(0, n, step, 0)


class Gather:
    def __init__(self, at, kv, zs, zr, ys, yr):
        self.at, self.kv, self.zs, self.zr, self.ys, self.yr = at, kv, zs, zr, ys, yr
        self.block = ZH * ROWS

    def z_copy(self, g, off, sending):
        at = self.at
        zh = at.zh if sending else mod(at.zh - off, ZH)
        ref = self.kv.at[g, :, rows_at((at.y * ZH + zh) * ROWS, ROWS), :]
        target = at.device(z=mod(at.zh + off, ZH) * ZL + at.zl)
        return rcopy(ref, ref, self.zs.at[g, off - 1], self.zr.at[g, off - 1], target)

    def y_copy(self, g, s, which, sending):
        at = self.at
        lag = s if sending else s + 1
        blk = mod(at.y - lag, Y) if which == 0 else mod(at.y + lag, Y)
        to = mod(at.y + 1, Y) if which == 0 else mod(at.y - 1, Y)
        ref = self.kv.at[g, which, rows_at(blk * self.block, self.block), :]
        return rcopy(ref, ref, self.ys.at[g, s, which], self.yr.at[g, s, which], at.device(y=to))

    def z_start(self, g):
        for off in range(1, ZH):
            self.z_copy(g, off, True).start()

    def z_wait(self, g):
        for off in range(1, ZH):
            self.z_copy(g, off, False).wait_recv()

    def y_start(self, g, s):
        for which in range(2):
            self.y_copy(g, s, which, True).start()

    def y_wait(self, g, s):
        for which in range(2):
            self.y_copy(g, s, which, False).wait_recv()

    def wait_sends(self, g):
        for off in range(1, ZH):
            self.z_copy(g, off, True).wait_send()
        for s in range(Y - 1):
            for which in range(2):
                self.y_copy(g, s, which, True).wait_send()


class Scatter:
    def __init__(self, at, tm, rb, zb, ss, sr, ws, wr):
        self.at, self.tm, self.rb, self.zb = at, tm, rb, zb
        self.ss, self.sr, self.ws, self.wr = ss, sr, ws, wr
        self.block = ZH * ROWS

    def rows(self, s, which):
        at = self.at
        blk = mod(at.y - 1 - s + Y, Y) if which == 0 else mod(at.y + 1 + s, Y)
        return rows_at(blk * self.block, self.block)

    def y_copy(self, g, s, which):
        at = self.at
        to = mod(at.y + 1, Y) if which == 0 else mod(at.y - 1, Y)
        return rcopy(self.tm.at[g, which, self.rows(s, which), :], self.rb.at[g, s, which],
                     self.ss.at[g, s, which], self.sr.at[g, s, which], at.device(y=to))

    def y_step(self, g, s):
        for which in range(2):
            if s > 0:
                self.y_copy(g, s - 1, which).wait_recv()
                rows = self.rows(s, which)
                total = self.tm[g, which, rows, :].astype(F32) + self.rb[g, s - 1, which].astype(F32)
                self.tm[g, which, rows, :] = total.astype(BF16)
            if s < Y - 1:
                self.y_copy(g, s, which).start()

    def z_copy(self, g, off):
        at = self.at
        zh = mod(at.zh + off, ZH)
        src = self.tm.at[g, :, rows_at((at.y * ZH + zh) * ROWS, ROWS), :]
        return rcopy(src, self.zb.at[g, off - 1], self.ws.at[g, off - 1], self.wr.at[g, off - 1],
                     at.device(z=zh * ZL + at.zl))

    def z_start(self, g):
        for off in range(1, ZH):
            self.z_copy(g, off).start()

    def finish(self, g, outs):
        at = self.at
        for off in range(1, ZH):
            self.z_copy(g, off).wait_recv()
        for which in range(2):
            total = self.tm[g, which, rows_at(at.r * ROWS, ROWS), :].astype(F32)
            for off in range(1, ZH):
                total += self.zb[g, off - 1, which].astype(F32)
            outs[which][:, pl.ds(pl.multiple_of(g * HD, HD), HD)] = total.astype(BF16)

    def wait_sends(self, g):
        for off in range(1, ZH):
            self.z_copy(g, off).wait_send()
        for s in range(Y - 1):
            for which in range(2):
                self.y_copy(g, s, which).wait_send()


class Reduce:
    def __init__(self, at, src, out, rc, rx, ry, rz, part, send, recv):
        self.at, self.src, self.out = at, src, out
        self.rc, self.rx, self.ry, self.rz, self.part = rc, rx, ry, rz, part
        self.send, self.recv = send, recv
        self.half = Y * LANES
        self.pending = []

    def rows(self, x):
        return pl.ds(pl.multiple_of(x * 16, 16), 16)

    def lanes(self, core, y=None):
        if y is None:
            return pl.ds(pl.multiple_of(core * self.half, LANES), self.half)
        return pl.ds(pl.multiple_of(core * self.half + y * LANES, LANES), LANES)

    def core_copy(self):
        at = self.at
        other = mod(at.core + 1, C)
        return rcopy(self.src.at[:, self.lanes(other)], self.rc, self.send.at[0, 0], self.recv.at[0, 0],
                     at.device(core=other))

    def x_copy(self, off):
        x = mod(self.at.x + off, X)
        return rcopy(self.part.at[self.rows(x), :], self.rx.at[off - 1], self.send.at[1, off - 1],
                     self.recv.at[1, off - 1], self.at.device(x=x))

    def y_copy(self, off):
        y = mod(self.at.y + off, Y)
        return rcopy(self.part.at[self.rows(self.at.x), pl.ds(pl.multiple_of(y * LANES, LANES), LANES)],
                     self.ry.at[off - 1], self.send.at[2, off - 1], self.recv.at[2, off - 1], self.at.device(y=y))

    def z_copy(self, off, sending):
        n = ZH * ZL
        z = self.at.z if sending else mod(self.at.z - off, n)
        return rcopy(self.rz.at[z], self.rz.at[z], self.send.at[3, off - 1], self.recv.at[3, off - 1],
                     self.at.device(z=mod(self.at.z + off, n)))

    def y_back(self, off, sending):
        y = self.at.y if sending else mod(self.at.y - off, Y)
        ref = self.out.at[self.rows(self.at.x), self.lanes(self.at.core, y)]
        return rcopy(ref, ref, self.send.at[4, off - 1], self.recv.at[4, off - 1],
                     self.at.device(y=mod(self.at.y + off, Y)))

    def x_back(self, off, sending):
        x = self.at.x if sending else mod(self.at.x - off, X)
        ref = self.out.at[self.rows(x), self.lanes(self.at.core)]
        return rcopy(ref, ref, self.send.at[5, off - 1], self.recv.at[5, off - 1],
                     self.at.device(x=mod(self.at.x + off, X)))

    def core_back(self, sending):
        core = self.at.core if sending else mod(self.at.core + 1, C)
        ref = self.out.at[:, self.lanes(core)]
        return rcopy(ref, ref, self.send.at[6, 0], self.recv.at[6, 0], self.at.device(core=mod(self.at.core + 1, C)))

    def steps(self):
        at = self.at
        n = ZH * ZL
        mine = lambda: (self.rows(at.x), pl.ds(pl.multiple_of(at.y * LANES, LANES), LANES))

        def core_start():
            self.core_copy().start()

        def x_start():
            self.core_copy().wait_recv()
            self.part[...] = (self.src[:, self.lanes(at.core)].astype(F32) + self.rc[...].astype(F32)).astype(BF16)
            for off in range(1, X):
                self.x_copy(off).start()

        def y_start():
            total = self.part[self.rows(at.x), :].astype(F32)
            for off in range(1, X):
                self.x_copy(off).wait_recv()
                total += self.rx[off - 1].astype(F32)
            self.part[self.rows(at.x), :] = total.astype(BF16)
            for off in range(1, Y):
                self.y_copy(off).start()

        def z_start():
            rows, lanes = mine()
            total = self.part[rows, lanes].astype(F32)
            for off in range(1, Y):
                self.y_copy(off).wait_recv()
                total += self.ry[off - 1].astype(F32)
            self.rz[at.z] = total.astype(BF16)
            for off in range(1, n):
                self.z_copy(off, True).start()

        def back_y():
            for off in range(1, n):
                self.z_copy(off, False).wait_recv()
            total = self.rz[0].astype(F32)
            for z in range(1, n):
                total += self.rz[z].astype(F32)
            self.out[self.rows(at.x), self.lanes(at.core, at.y)] = total.astype(BF16)
            for off in range(1, Y):
                self.y_back(off, True).start()

        def back_x():
            for off in range(1, Y):
                self.y_back(off, False).wait_recv()
            for off in range(1, X):
                self.x_back(off, True).start()

        def back_core():
            for off in range(1, X):
                self.x_back(off, False).wait_recv()
            self.core_back(True).start()

        def end():
            self.core_back(False).wait_recv()
            self.core_copy().wait_send()
            self.core_back(True).wait_send()
            for off in range(1, X):
                self.x_copy(off).wait_send()
                self.x_back(off, True).wait_send()
            for off in range(1, Y):
                self.y_copy(off).wait_send()
                self.y_back(off, True).wait_send()
            for off in range(1, n):
                self.z_copy(off, True).wait_send()

        return [core_start, x_start, y_start, z_start, back_y, back_x, back_core, end]


def attention(g, at, length, refs, kv, tm, scr):
    (pq, rq, pdo, rdo, po, ro, rk, rv) = refs
    (qs, dos, s_scr, e_scr, t_scr, dq_scr, rdk, rdv, hid, up_w, mid_t, ar_src) = scr
    chunk = ZH * ROWS
    prefix = Y * chunk
    base = pl.multiple_of(g * GROUP_LANES, HD)
    head_lanes = pl.ds(pl.multiple_of(g * HD, HD), HD)
    alive = lax.broadcasted_iota(jnp.int32, (ROWS, HD), 0) < length

    deltas = []
    for h in range(GROUPS):
        lanes = pl.ds(pl.multiple_of(base + h * HD, HD), HD)
        top, low = pl.ds(2 * h * ROWS, ROWS), pl.ds((2 * h + 1) * ROWS, ROWS)
        qs[top, :] = pq[:, lanes]
        qs[low, :] = rq[:, lanes]
        grad_top = pdo[:, lanes].astype(F32)
        grad_low = jnp.where(alive, rdo[:, lanes].astype(F32), 0.0)
        dos[top, :] = grad_top.astype(BF16)
        dos[low, :] = grad_low.astype(BF16)
        both = jnp.concatenate([grad_top * po[:, lanes].astype(F32), grad_low * ro[:, lanes].astype(F32)], axis=0)
        deltas.append(jnp.sum(both.T, axis=0, keepdims=True))
    delta = jnp.concatenate(deltas, axis=1)
    q, do = qs[...], dos[...]

    lane = lax.broadcasted_iota(jnp.int32, (1, QL), 1)
    in_head = lax.rem(lane, 2 * ROWS)
    limit = jnp.where(in_head < ROWS, at.r * ROWS + in_head, prefix)
    own_limit = in_head - ROWS
    row = lax.broadcasted_iota(jnp.int32, (chunk, QL), 0)
    own_row = lax.broadcasted_iota(jnp.int32, (ROWS, QL), 0)

    def top8(s, op):
        return op(s.reshape(s.shape[0] // 8, 8, QL), axis=0)

    s = jnp.where(own_row <= own_limit, nt(rk[:, head_lanes], q), -jnp.inf)
    s_scr[pl.ds(prefix, ROWS), :] = s

    def scores(c, m8):
        at_c = rows_at(c * chunk, chunk)
        s = jnp.where(row + c * chunk <= limit, nt(kv[g, 0, at_c, :], q), -jnp.inf)
        s_scr[at_c, :] = s
        return jnp.maximum(m8, top8(s, jnp.max))

    m8 = lax.fori_loop(0, Y, scores, top8(s, jnp.max))
    m = jnp.max(m8, axis=0, keepdims=True) * (SCALE * LOG2E)

    def weights(at_c, k, v):
        e = jnp.exp2(s_scr[at_c, :] * (SCALE * LOG2E) - m)
        t = (e * (nt(v, do) - delta)).astype(BF16)
        e_scr[at_c, :] = e.astype(BF16)
        t_scr[at_c, :] = t
        return top8(e, jnp.sum), tn(k, t)

    def back(c, carry):
        at_c = rows_at(c * chunk, chunk)
        l8, dq = weights(at_c, kv[g, 0, at_c, :], kv[g, 1, at_c, :])
        return carry[0] + l8, carry[1] + dq

    l8, dq = lax.fori_loop(0, Y, back, weights(pl.ds(prefix, ROWS), rk[:, head_lanes], rv[:, head_lanes]))
    inv = 1.0 / jnp.sum(l8, axis=0, keepdims=True)
    inv_col = jnp.concatenate(
        [jnp.broadcast_to(inv[:, h * HD:(h + 1) * HD], (HD, HD)).T for h in range(GROUPS)], axis=0)
    q_n = (q.astype(F32) * (inv_col * SCALE)).astype(BF16)
    do_n = (do.astype(F32) * inv_col).astype(BF16)
    dq_low = (dq * (inv * SCALE)).astype(BF16)

    def terms(c, carry):
        at_c = rows_at(c * chunk, chunk)
        tm[g, 0, at_c, :] = nn(t_scr[at_c, :], q_n).astype(BF16)
        tm[g, 1, at_c, :] = nn(e_scr[at_c, :], do_n).astype(BF16)
        return carry

    lax.fori_loop(0, Y, terms, 0)
    own = pl.ds(prefix, ROWS)
    rdk[:, head_lanes] = nn(t_scr[own, :], q_n).astype(BF16)
    rdv[:, head_lanes] = nn(e_scr[own, :], do_n).astype(BF16)

    hidden = hid[...]
    for h in range(GROUPS):
        lanes = pl.ds(pl.multiple_of(base + h * HD, HD), HD)
        part = dq_low[:, h * HD:(h + 1) * HD]
        hidden += nn(up_w[:, lanes], part)
        ar_src[:, pl.ds(pl.multiple_of(10 * LANES + base + h * HD, HD), HD)] = nt(mid_t, part).astype(BF16)
    hid[...] = hidden


def down_terms(hid, px, rx, ar_src):
    hidden = hid[...].astype(BF16)
    width = px.shape[1]
    for j in range(0, width, LANES):
        lanes = slice(j, j + LANES)
        ar_src[:, lanes] = (nn(hidden[:, :ROWS], px[:, lanes]) + nn(hidden[:, ROWS:], rx[:, lanes])).astype(BF16)
    ar_src[:, 15 * LANES:] = jnp.zeros((RANK, LANES), BF16)


def kernel(length_ref, pk, pv, rk, rv, pq, rq, pdo, rdo, po, ro, px, rx, pm, rm, up_w,
           pdk, pdv, rdk, rdv, total,
           kv, tm, rb, zb, qs, dos, s_scr, e_scr, t_scr, dq_scr, hid, ar_src, rc, rx_b, ry, rz, part,
           zs, zr, ys, yr, ss, sr, ws, wr, asend, arecv):
    at = Place()
    gather = Gather(at, kv, zs, zr, ys, yr)
    scatter = Scatter(at, tm, rb, zb, ss, sr, ws, wr)
    reduce = Reduce(at, ar_src, total, rc, rx_b, ry, rz, part, asend, arecv)

    for g in range(KVH):
        kv[g, 0, rows_at(at.r * ROWS, ROWS), :] = pk[:, g * HD:(g + 1) * HD]
        kv[g, 1, rows_at(at.r * ROWS, ROWS), :] = pv[:, g * HD:(g + 1) * HD]
    entry_barrier(at)
    each(KVH, gather.z_start)

    def first(g):
        gather.z_wait(g)
        gather.y_start(g, 0)
    each(KVH, first)
    for s in range(1, Y - 1):
        def pass_on(g, s=s):
            gather.y_wait(g, s - 1)
            gather.y_start(g, s)
        each(KVH, pass_on)
    each(KVH, lambda g: gather.y_wait(g, Y - 2))

    hid[...] = jnp.zeros_like(hid)
    mid_t = jnp.concatenate([pm[...].astype(F32).T, rm[...].astype(F32).T], axis=1).astype(BF16)
    refs = (pq, rq, pdo, rdo, po, ro, rk, rv)
    scr = (qs, dos, s_scr, e_scr, t_scr, dq_scr, rdk, rdv, hid, up_w, mid_t, ar_src)
    each(KVH, lambda g: attention(g, at, length_ref[0, 0], refs, kv, tm, scr))
    down_terms(hid, px, rx, ar_src)

    reduce_steps = reduce.steps()
    for s in range(Y):
        if s < len(reduce_steps):
            reduce_steps[s]()
        each(KVH, lambda g, s=s: scatter.y_step(g, s))
    each(KVH, scatter.z_start)
    for step in reduce_steps[Y:]:
        step()
    each(KVH, lambda g: scatter.finish(g, (pdk, pdv)))
    each(KVH, gather.wait_sends)
    each(KVH, scatter.wait_sends)


def local(
    prefix_input, prefix_query_rows, prefix_key_rows, prefix_value_rows, prefix_output, prefix_output_grad,
    prefix_middle, response_input, response_query, response_key, response_value, response_output,
    response_output_grad, response_middle, lengths, adapter_up_weight,
):
    prefix = Y * ZH * ROWS
    width = 2 * Y * LANES
    vmem = pl.BlockSpec(memory_space=pltpu.VMEM)
    kv_width = KVH * HD
    dma = pltpu.SemaphoreType.DMA
    most = max(Y, ZH * ZL, X) - 1
    small = jax.ShapeDtypeStruct((ROWS, kv_width), BF16)
    outs = pl.pallas_call(
        kernel,
        out_shape=[small, small, small, small, jax.ShapeDtypeStruct((RANK, width), BF16)],
        in_specs=[pl.BlockSpec(memory_space=pltpu.SMEM)] + [vmem] * 15,
        out_specs=[vmem] * 5,
        scratch_shapes=[
            pltpu.VMEM((KVH, 2, prefix, HD), BF16),
            pltpu.VMEM((KVH, 2, prefix, HD), BF16),
            pltpu.VMEM((KVH, Y - 1, 2, ZH * ROWS, HD), BF16),
            pltpu.VMEM((KVH, ZH - 1, 2, ROWS, HD), BF16),
            pltpu.VMEM((QL, HD), BF16),
            pltpu.VMEM((QL, HD), BF16),
            pltpu.VMEM((prefix + ROWS, QL), F32),
            pltpu.VMEM((prefix + ROWS, QL), BF16),
            pltpu.VMEM((prefix + ROWS, QL), BF16),
            pltpu.VMEM((8, HD), F32),
            pltpu.VMEM((RANK, 2 * ROWS), F32),
            pltpu.VMEM((RANK, width), BF16),
            pltpu.VMEM((RANK, width // 2), BF16),
            pltpu.VMEM((X - 1, 16, width // 2), BF16),
            pltpu.VMEM((Y - 1, 16, LANES), BF16),
            pltpu.VMEM((ZH * ZL, 16, LANES), BF16),
            pltpu.VMEM((RANK, width // 2), BF16),
            dma((KVH, ZH - 1)), dma((KVH, ZH - 1)),
            dma((KVH, Y - 1, 2)), dma((KVH, Y - 1, 2)),
            dma((KVH, Y - 1, 2)), dma((KVH, Y - 1, 2)),
            dma((KVH, ZH - 1)), dma((KVH, ZH - 1)),
            dma((7, most)), dma((7, most)),
        ],
        compiler_params=pltpu.CompilerParams(
            collective_id=0, has_side_effects=True, vmem_limit_bytes=56 * 1024 * 1024),
    )(
        lengths, prefix_key_rows[0], prefix_value_rows[0], response_key[0, 0], response_value[0, 0],
        prefix_query_rows[0], response_query[0, 0], prefix_output_grad[0], response_output_grad[0, 0],
        prefix_output[0], response_output[0, 0], prefix_input[0], response_input[0, 0],
        prefix_middle[0], response_middle[0, 0], adapter_up_weight,
    )
    dkey, dvalue, resp_dkey, resp_dvalue, total = outs
    down = 2.0 * total[:, :10 * LANES].astype(F32)
    up = 2.0 * total[:, 10 * LANES:15 * LANES].astype(F32)
    return dkey[None], dvalue[None], resp_dkey[None, None], resp_dvalue[None, None], down.T, up


def solution(mesh):
    rows, slots = P("prompt", "resp", None), P("prompt", "resp", None, None)
    return jax.shard_map(
        local,
        mesh=mesh,
        in_specs=(rows,) * 7 + (slots,) * 7 + (P("prompt", "resp"), P()),
        out_specs=(rows, rows, slots, slots, P(), P()),
        check_vma=False,
    )
```

```python
import functools
import math

import jax
import jax.numpy as jnp
from jax import lax
from jax.experimental import pallas as pl
from jax.experimental.pallas import tpu as pltpu
from jax.sharding import PartitionSpec as P

ZL, X, C, Y, ZH = 2, 4, 2, 8, 4
HD = 128
ROWS = 64
KVH = 4
PAIR = 2
GROUPS = 5
RANK = 64
GROUP_LANES = GROUPS * HD
CHUNK = 4 * HD
PIECE = C * Y * CHUNK
PIECES = 1
FAR = 9
DOWN = KVH * GROUP_LANES
DOWN_END = DOWN + 5120
WIDTH = PIECES * PIECE
QL = 2 * ROWS * GROUPS
SCALE = HD ** -0.5
LOG2E = math.log2(math.e)
F32 = jnp.float32
BF16 = jnp.bfloat16
MESH = pl.DeviceIdType.MESH


def mod(a, n):
    return lax.rem(a + n, n)


def nt(a, b):
    return lax.dot_general(a, b, (((1,), (1,)), ((), ())), preferred_element_type=F32)


def nn(a, b):
    return lax.dot_general(a, b, (((1,), (0,)), ((), ())), preferred_element_type=F32)


def tn(a, b):
    return lax.dot_general(a, b, (((0,), (0,)), ((), ())), preferred_element_type=F32)


class Place:
    def __init__(self):
        p, r = lax.axis_index("prompt"), lax.axis_index("resp")
        self.p, self.r = p, r
        self.core = lax.rem(p, C)
        self.x = lax.rem(lax.div(p, C), X)
        self.zl = lax.div(p, C * X)
        self.y = lax.div(r, ZH)
        self.zh = lax.rem(r, ZH)
        self.z = self.zh * ZL + self.zl

    def device(self, core=None, x=None, y=None, z=None):
        core = self.core if core is None else core
        x = self.x if x is None else x
        y = self.y if y is None else y
        z = self.z if z is None else z
        zl, zh = lax.rem(z, ZL), lax.div(z, ZL)
        return {"prompt": (zl * X + x) * C + core, "resp": y * ZH + zh}


def entry_barrier(at):
    barrier = pltpu.get_barrier_semaphore()
    count = 0
    for off in range(1, C):
        pl.semaphore_signal(barrier, inc=1, device_id=at.device(core=mod(at.core + off, C)), device_id_type=MESH)
        count += 1
    for off in range(1, X):
        pl.semaphore_signal(barrier, inc=1, device_id=at.device(x=mod(at.x + off, X)), device_id_type=MESH)
        count += 1
    for off in range(1, Y):
        pl.semaphore_signal(barrier, inc=1, device_id=at.device(y=mod(at.y + off, Y)), device_id_type=MESH)
        count += 1
    for off in range(1, ZH * ZL):
        pl.semaphore_signal(barrier, inc=1, device_id=at.device(z=mod(at.z + off, ZH * ZL)), device_id_type=MESH)
        count += 1
    return lambda: pl.semaphore_wait(barrier, count)


def rcopy(src, dst, send, recv, device):
    return pltpu.make_async_remote_copy(
        src_ref=src, dst_ref=dst, send_sem=send, recv_sem=recv, device_id=device, device_id_type=MESH)


def rows_at(start, count):
    return pl.ds(pl.multiple_of(start, ROWS), count)


def when(condition, body):
    pl.when(condition)(body)


def each(n, body):
    def step(i, carry):
        body(i)
        return carry
    lax.fori_loop(0, n, step, 0)


def hops(which, way):
    return Y // 2 if which == way else Y - 1 - Y // 2


def chains(turn):
    for which in range(2):
        for way in range(2):
            turn(which, way, hops(which, way), 1 if way == 0 else -1)


class Gather:
    def __init__(self, at, kv, zs, zr, ys, yr):
        self.at, self.kv, self.zs, self.zr, self.ys, self.yr = at, kv, zs, zr, ys, yr

    def z_copy(self, h, off, sending):
        at = self.at
        zh = at.zh if sending else mod(at.zh - off, ZH)
        ref = self.kv.at[h, :, at.y, zh]
        target = at.device(z=mod(at.zh + off, ZH) * ZL + at.zl)
        return rcopy(ref, ref, self.zs.at[h, off - 1], self.zr.at[h, off - 1], target)

    def z_start(self, h):
        for off in range(1, ZH):
            self.z_copy(h, off, True).start()

    def z_wait(self, h):
        for off in range(1, ZH):
            self.z_copy(h, off, False).wait_recv()

    def y_copy(self, h, s, which, way, sign, sending):
        at = self.at
        lag = s if sending else s + 1
        ref = self.kv.at[h, which, mod(at.y - sign * lag + Y, Y)]
        return rcopy(ref, ref, self.ys.at[h, s, which, way], self.yr.at[h, s, which, way],
                     at.device(y=mod(at.y + sign, Y)))

    def y_step(self, h, s):
        def turn(which, way, count, sign):
            when((s > 0) & (s <= count), lambda: self.y_copy(h, s - 1, which, way, sign, False).wait_recv())
            when(s < count, lambda: self.y_copy(h, s, which, way, sign, True).start())
        chains(turn)

    def wait_sends(self, h):
        for off in range(1, ZH):
            self.z_copy(h, off, True).wait_send()

        def turn(which, way, count, sign):
            each(count, lambda s: self.y_copy(h, s, which, way, sign, True).wait_send())
        chains(turn)


class Scatter:
    def __init__(self, at, tm, rb, zb, ss, sr, ws, wr, outs):
        self.at, self.tm, self.rb, self.zb = at, tm, rb, zb
        self.ss, self.sr, self.ws, self.wr = ss, sr, ws, wr
        self.outs = outs

    def y_ref(self, h, s, which, count, sign):
        return self.tm.at[h, which, mod(self.at.y + sign * (count - s) + Y, Y)]

    def y_copy(self, h, s, which, way, count, sign):
        return rcopy(self.y_ref(h, s, which, count, sign), self.rb.at[h, s, which, way],
                     self.ss.at[h, s, which, way], self.sr.at[h, s, which, way],
                     self.at.device(y=mod(self.at.y + sign, Y)))

    def y_step(self, h, s):
        def turn(which, way, count, sign):
            def receive():
                self.y_copy(h, s - 1, which, way, count, sign).wait_recv()
                ref = self.y_ref(h, s, which, count, sign)
                ref[...] = (ref[...].astype(F32) + self.rb[h, s - 1, which, way].astype(F32)).astype(BF16)
            when((s > 0) & (s <= count), receive)
            when(s < count, lambda: self.y_copy(h, s, which, way, count, sign).start())
        chains(turn)

    def z_copy(self, h, off):
        at = self.at
        zh = mod(at.zh + off, ZH)
        return rcopy(self.tm.at[h, :, at.y, zh], self.zb.at[h, off - 1], self.ws.at[h, off - 1],
                     self.wr.at[h, off - 1], at.device(z=zh * ZL + at.zl))

    def z_start(self, h):
        for off in range(1, ZH):
            self.z_copy(h, off).start()

    def finish(self, h):
        at = self.at
        for off in range(1, ZH):
            self.z_copy(h, off).wait_recv()
        for which in range(2):
            total = self.tm[h, which, at.y, at.zh].astype(F32)
            for off in range(1, ZH):
                total += self.zb[h, off - 1, which].astype(F32)
            self.outs[which][:, h * HD:(h + 1) * HD] = total.astype(BF16)

    def wait_sends(self, h):
        for off in range(1, ZH):
            self.z_copy(h, off).wait_send()

        def turn(which, way, count, sign):
            each(count, lambda s: self.y_copy(h, s, which, way, count, sign).wait_send())
        chains(turn)


class Reduce:
    def __init__(self, at, src, out, rc, rx, ry, rz, part, send, recv):
        self.at, self.src, self.out = at, src, out
        self.rc, self.rx, self.ry, self.rz, self.part = rc, rx, ry, rz, part
        self.send, self.recv = send, recv
        self.n = ZH * ZL

    def rows(self, x):
        return pl.ds(pl.multiple_of(x * 16, 16), 16)

    def half(self, i, core):
        return pl.ds(pl.multiple_of(i * PIECE + core * (PIECE // 2), HD), PIECE // 2)

    def lanes(self, i, core, y):
        return pl.ds(pl.multiple_of(i * PIECE + core * (PIECE // 2) + y * CHUNK, HD), CHUNK)

    def chunk(self, y):
        return pl.ds(pl.multiple_of(y * CHUNK, HD), CHUNK)

    def sems(self, i, step, off):
        return self.send.at[i, step, off - 1], self.recv.at[i, step, off - 1]

    def core_copy(self, i):
        other = mod(self.at.core + 1, C)
        return rcopy(self.src.at[:, self.half(i, other)], self.rc.at[i], *self.sems(i, 0, 1),
                     self.at.device(core=other))

    def x_copy(self, i, off):
        x = mod(self.at.x + off, X)
        return rcopy(self.part.at[i, self.rows(x), :], self.rx.at[i, off - 1], *self.sems(i, 1, off),
                     self.at.device(x=x))

    def y_copy(self, i, off):
        y = mod(self.at.y + off, Y)
        return rcopy(self.part.at[i, self.rows(self.at.x), self.chunk(y)], self.ry.at[i, off - 1],
                     *self.sems(i, 2, off), self.at.device(y=y))

    def z_copy(self, i, off, sending):
        z = self.at.z if sending else mod(self.at.z - off, self.n)
        return rcopy(self.rz.at[i, z], self.rz.at[i, z], *self.sems(i, 3, off),
                     self.at.device(z=mod(self.at.z + off, self.n)))

    def y_back(self, i, off, sending):
        y = self.at.y if sending else mod(self.at.y - off, Y)
        ref = self.out.at[self.rows(self.at.x), self.lanes(i, self.at.core, y)]
        return rcopy(ref, ref, *self.sems(i, 4, off), self.at.device(y=mod(self.at.y + off, Y)))

    def x_back(self, i, off, sending):
        x = self.at.x if sending else mod(self.at.x - off, X)
        ref = self.out.at[self.rows(x), self.half(i, self.at.core)]
        return rcopy(ref, ref, *self.sems(i, 5, off), self.at.device(x=mod(self.at.x + off, X)))

    def core_back(self, i, sending):
        core = self.at.core if sending else mod(self.at.core + 1, C)
        ref = self.out.at[:, self.half(i, core)]
        return rcopy(ref, ref, *self.sems(i, 6, 1), self.at.device(core=mod(self.at.core + 1, C)))

    def step(self, i, k):
        at = self.at
        if k == 0:
            self.core_copy(i).start()
        if k == 1:
            self.core_copy(i).wait_recv()
            self.part[i] = (self.src[:, self.half(i, at.core)].astype(F32) + self.rc[i].astype(F32)).astype(BF16)
            for off in range(1, X):
                self.x_copy(i, off).start()
        if k == 2:
            total = self.part[i, self.rows(at.x), :].astype(F32)
            for off in range(1, X):
                self.x_copy(i, off).wait_recv()
                total += self.rx[i, off - 1].astype(F32)
            self.part[i, self.rows(at.x), :] = total.astype(BF16)
            for off in range(1, Y):
                self.y_copy(i, off).start()
        if k == 3:
            total = self.part[i, self.rows(at.x), self.chunk(at.y)].astype(F32)
            for off in range(1, Y):
                self.y_copy(i, off).wait_recv()
                total += self.ry[i, off - 1].astype(F32)
            self.rz[i, at.z] = total.astype(BF16)
            for off in range(1, self.n):
                self.z_copy(i, off, True).start()
        if k == 4:
            for off in range(1, self.n):
                self.z_copy(i, off, False).wait_recv()
            total = self.rz[i, 0].astype(F32)
            for z in range(1, self.n):
                total += self.rz[i, z].astype(F32)
            self.out[self.rows(at.x), self.lanes(i, at.core, at.y)] = total.astype(BF16)
            for off in range(1, Y):
                self.y_back(i, off, True).start()
        if k == 5:
            for off in range(1, Y):
                self.y_back(i, off, False).wait_recv()
            for off in range(1, X):
                self.x_back(i, off, True).start()
        if k == 6:
            for off in range(1, X):
                self.x_back(i, off, False).wait_recv()
            self.core_back(i, True).start()
        if k == 7:
            self.core_back(i, False).wait_recv()

    def wait_sends(self, i):
        self.core_copy(i).wait_send()
        self.core_back(i, True).wait_send()
        for off in range(1, X):
            self.x_copy(i, off).wait_send()
            self.x_back(i, off, True).wait_send()
        for off in range(1, Y):
            self.y_copy(i, off).wait_send()
            self.y_back(i, off, True).wait_send()
        for off in range(1, self.n):
            self.z_copy(i, off, True).wait_send()


class Attention:
    def __init__(self, at, length, refs, kv, tm, scr):
        self.at, self.length, self.kv, self.tm = at, length, kv, tm
        (self.pq, self.rq, self.pdo, self.rdo, self.po, self.ro, self.rk, self.rv, self.up_w, self.mid_t) = refs
        (self.qs, self.dos, self.delta, self.s, self.e, self.t, self.hid, self.ar_src, self.rdk, self.rdv) = scr
        self.chunk = PAIR * ZH * ROWS
        self.prefix = Y * ZH * ROWS
        lane = lax.broadcasted_iota(jnp.int32, (1, QL), 1)
        self.in_head = lax.rem(lane, 2 * ROWS)

    def keys(self, h, which, c):
        return self.kv[h, which, pl.ds(c * PAIR, PAIR)].reshape(self.chunk, HD)

    def lanes(self, h):
        return pl.ds(pl.multiple_of(h * HD, HD), HD)

    def q_lanes(self, h, i):
        return pl.ds(pl.multiple_of(h * GROUP_LANES + i * HD, HD), HD)

    def rows_of(self, c):
        return pl.ds(pl.multiple_of(c * self.chunk, self.chunk), self.chunk)

    def prepare(self, h):
        alive = lax.broadcasted_iota(jnp.int32, (ROWS, HD), 0) < self.length
        for i in range(GROUPS):
            lanes = self.q_lanes(h, i)
            top, low = pl.ds(2 * i * ROWS, ROWS), pl.ds((2 * i + 1) * ROWS, ROWS)
            self.qs[h, top, :] = self.pq[:, lanes]
            self.qs[h, low, :] = self.rq[:, lanes]
            grad_top = self.pdo[:, lanes].astype(F32)
            grad_low = jnp.where(alive, self.rdo[:, lanes].astype(F32), 0.0)
            self.dos[h, top, :] = grad_top.astype(BF16)
            self.dos[h, low, :] = grad_low.astype(BF16)
            both = jnp.concatenate(
                [grad_top * self.po[:, lanes].astype(F32), grad_low * self.ro[:, lanes].astype(F32)], axis=0)
            self.delta[h, :, i * HD:(i + 1) * HD] = jnp.sum(both.T, axis=0, keepdims=True)

    def top8(self, s, op):
        return op(s.reshape(s.shape[0] // 8, 8, QL), axis=0)

    def scores(self, h, tick):
        q = self.qs[h]
        limit = jnp.where(self.in_head < ROWS, self.at.r * ROWS + self.in_head, self.prefix)
        own_row = lax.broadcasted_iota(jnp.int32, (ROWS, QL), 0)
        row = lax.broadcasted_iota(jnp.int32, (self.chunk, QL), 0)
        s = jnp.where(own_row <= self.in_head - ROWS, nt(self.rk[:, self.lanes(h)], q), -jnp.inf)
        self.s[pl.ds(self.prefix, ROWS), :] = s

        def body(c, m8):
            tick(c)
            s = jnp.where(row + c * self.chunk <= limit, nt(self.keys(h, 0, c), q), -jnp.inf)
            self.s[self.rows_of(c), :] = s
            return jnp.maximum(m8, self.top8(s, jnp.max))

        m8 = lax.fori_loop(0, Y // PAIR, body, self.top8(s, jnp.max))
        return jnp.max(m8, axis=0, keepdims=True) * (SCALE * LOG2E)

    def weights(self, h, slot, m, tick):
        do, delta = self.dos[h], self.delta[h]

        def part(at_c, k, v):
            e = jnp.exp2(self.s[at_c, :] * (SCALE * LOG2E) - m)
            t = (e * (nt(v, do) - delta)).astype(BF16)
            self.e[slot, at_c, :] = e.astype(BF16)
            self.t[slot, at_c, :] = t
            return self.top8(e, jnp.sum), tn(k, t)

        def body(c, carry):
            tick(c)
            l8, dq = part(self.rows_of(c), self.keys(h, 0, c), self.keys(h, 1, c))
            return carry[0] + l8, carry[1] + dq

        own = part(pl.ds(self.prefix, ROWS), self.rk[:, self.lanes(h)], self.rv[:, self.lanes(h)])
        l8, dq = lax.fori_loop(0, Y // PAIR, body, own)
        inv = 1.0 / jnp.sum(l8, axis=0, keepdims=True)
        inv_col = jnp.concatenate(
            [jnp.broadcast_to(inv[:, i * HD:(i + 1) * HD], (HD, HD)).T for i in range(GROUPS)], axis=0)
        self.qs[h] = (self.qs[h].astype(F32) * (inv_col * SCALE)).astype(BF16)
        self.dos[h] = (self.dos[h].astype(F32) * inv_col).astype(BF16)
        dq_low = (dq * (inv * SCALE)).astype(BF16)
        hidden = self.hid[...]
        for i in range(GROUPS):
            piece = dq_low[:, i * HD:(i + 1) * HD]
            hidden += nn(self.up_w[:, self.q_lanes(h, i)], piece)
            lanes = self.q_lanes(h, i)
            self.ar_src[:, lanes] = nt(self.mid_t[...], piece).astype(BF16)
        self.hid[...] = hidden

    def terms(self, h, slot, tick):
        q, do = self.qs[h], self.dos[h]

        def body(c, carry):
            tick(c)
            at_c = self.rows_of(c)
            shape = (PAIR, ZH, ROWS, HD)
            self.tm[h, 0, pl.ds(c * PAIR, PAIR)] = nn(self.t[slot, at_c, :], q).astype(BF16).reshape(shape)
            self.tm[h, 1, pl.ds(c * PAIR, PAIR)] = nn(self.e[slot, at_c, :], do).astype(BF16).reshape(shape)
            return carry

        lax.fori_loop(0, Y // PAIR, body, 0)
        own = pl.ds(self.prefix, ROWS)
        self.rdk[:, self.lanes(h)] = nn(self.t[slot, own, :], q).astype(BF16)
        self.rdv[:, self.lanes(h)] = nn(self.e[slot, own, :], do).astype(BF16)


def down_terms(hid, px, rx, ar_src):
    hidden = hid[...].astype(BF16)
    for j in range(0, DOWN_END - DOWN, 512):
        lanes = slice(j, j + 512)
        ar_src[:, DOWN + j:DOWN + j + 512] = (
            nn(hidden[:, :ROWS], px[:, lanes]) + nn(hidden[:, ROWS:], rx[:, lanes])).astype(BF16)


def kernel(length_ref, pk, pv, rk, rv, pm, rm, *rest):
    far, rest = rest[:FAR], rest[FAR:]
    (pdk, pdv, rdk, rdv, total), rest = rest[:5], rest[5:]
    near, rest = rest[:FAR], rest[FAR:]
    (kv, tm, rb, zb, qs, dos, delta, s_scr, e_scr, t_scr, hid, mid_t, ar_src, rc, rx_b, ry, rz, part,
     gzs, gzr, gys, gyr, sys, syr, szs, szr, asend, arecv, loaded) = rest
    pq, rq, pdo, rdo, po, ro, up_w, px, rx = near
    at = Place()
    gather = Gather(at, kv, gzs, gzr, gys, gyr)
    scatter = Scatter(at, tm, rb, zb, sys, syr, szs, szr, (pdk, pdv))
    reduce = Reduce(at, ar_src, total, rc, rx_b, ry, rz, part, asend, arecv)
    refs = (pq, rq, pdo, rdo, po, ro, rk, rv, up_w, mid_t)
    scr = (qs, dos, delta, s_scr, e_scr, t_scr, hid, ar_src, rdk, rdv)
    attention = Attention(at, length_ref[0, 0], refs, kv, tm, scr)
    parts = Y // PAIR
    last = Y // 2

    everyone_in = entry_barrier(at)
    loads = [pltpu.make_async_copy(far[i], near[i], loaded.at[i]) for i in range(FAR)]
    for load in loads:
        load.start()
    for h in range(KVH):
        kv[h, 0, at.y, at.zh] = pk[:, h * HD:(h + 1) * HD]
        kv[h, 1, at.y, at.zh] = pv[:, h * HD:(h + 1) * HD]
    everyone_in()
    each(KVH, gather.z_start)
    hid[...] = jnp.zeros_like(hid)
    ar_src[:, DOWN_END:] = jnp.zeros((RANK, WIDTH - DOWN_END), BF16)
    mid_t[...] = jnp.concatenate([pm[...].astype(F32).T, rm[...].astype(F32).T], axis=1).astype(BF16)

    for load in loads:
        load.wait()

    def begin(h):
        gather.z_wait(h)
        gather.y_step(h, 0)
    each(2, begin)

    def first(s):
        attention.prepare(s)
        each(2, lambda h: gather.y_step(h, s + 1))
    each(last, first)
    each(2, lambda i: begin(i + 2))

    def second(h):
        def tick(unit):
            def at_part(c):
                slot = (h * 3 + unit) * parts + c

                def events():
                    s = lax.div(slot, 5)
                    each(2, lambda i: gather.y_step(i + 2, s))
                when((lax.rem(slot, 5) == 0) & (slot > 0), events)
                when(slot == 17, lambda: scatter.y_step(0, 0))
            return at_part
        m = attention.scores(h, tick(0))
        attention.weights(h, h, m, tick(1))
        attention.terms(h, h, tick(2))
    each(2, second)

    def third(i):
        def tick(unit):
            def at_part(c):
                slot = (i * 2 + unit) * parts + c

                def events():
                    s = lax.div(slot, 8)
                    scatter.y_step(0, s + 1)
                    scatter.y_step(1, s)
                when(lax.rem(slot, 8) == 0, events)
            return at_part
        m = attention.scores(i + 2, tick(0))
        attention.weights(i + 2, i, m, tick(1))
    each(2, third)

    def sums(k):
        each(PIECES, lambda i: reduce.step(i, k))

    down_terms(hid, px, rx, ar_src)
    sums(0)
    attention.terms(2, 0, lambda c: None)
    scatter.y_step(0, 3)
    scatter.y_step(1, 2)
    scatter.y_step(2, 0)
    sums(1)
    attention.terms(3, 1, lambda c: None)
    scatter.y_step(3, 0)
    scatter.y_step(0, 4)
    scatter.z_start(0)
    sums(2)
    scatter.y_step(1, 3)
    scatter.y_step(2, 1)
    sums(3)
    scatter.y_step(3, 1)
    scatter.y_step(1, 4)
    scatter.z_start(1)
    sums(4)
    scatter.y_step(2, 2)
    scatter.y_step(3, 2)
    sums(5)
    scatter.y_step(2, 3)
    scatter.y_step(3, 3)
    sums(6)
    scatter.y_step(2, 4)
    scatter.z_start(2)
    scatter.y_step(3, 4)
    scatter.z_start(3)
    sums(7)
    for h in range(KVH):
        scatter.finish(h)
    each(KVH, gather.wait_sends)
    each(KVH, scatter.wait_sends)
    each(PIECES, reduce.wait_sends)


def results(total, pdk, pdv, rdk, rdv, down, up, *low):
    for src, dst in zip((pdk, pdv, rdk, rdv), low):
        dst[...] = src[...]
    down[...] = 2.0 * total[:, DOWN:DOWN_END].astype(F32)
    up[...] = 2.0 * total[:, :DOWN].astype(F32)


def local(
    prefix_input, prefix_query_rows, prefix_key_rows, prefix_value_rows, prefix_output, prefix_output_grad,
    prefix_middle, response_input, response_query, response_key, response_value, response_output,
    response_output_grad, response_middle, lengths, adapter_up_weight,
):
    prefix = Y * ZH * ROWS
    width = WIDTH
    vmem = pl.BlockSpec(memory_space=pltpu.VMEM)
    kv_width = KVH * HD
    dma = pltpu.SemaphoreType.DMA
    most = max(Y, ZH * ZL, X) - 1
    small = jax.ShapeDtypeStruct((ROWS, kv_width), BF16)
    far = (prefix_query_rows[0], response_query[0, 0], prefix_output_grad[0], response_output_grad[0, 0],
           prefix_output[0], response_output[0, 0], adapter_up_weight, prefix_input[0], response_input[0, 0])
    outs = pl.pallas_call(
        kernel,
        out_shape=[small, small, small, small, jax.ShapeDtypeStruct((RANK, width), BF16)],
        in_specs=[pl.BlockSpec(memory_space=pltpu.SMEM)] + [vmem] * 6 + [pl.BlockSpec(memory_space=pl.ANY)] * FAR,
        out_specs=[vmem] * 5,
        scratch_shapes=[pltpu.VMEM(a.shape, BF16) for a in far] + [
            pltpu.VMEM((KVH, 2, Y, ZH, ROWS, HD), BF16),
            pltpu.VMEM((KVH, 2, Y, ZH, ROWS, HD), BF16),
            pltpu.VMEM((KVH, Y // 2, 2, 2, ZH, ROWS, HD), BF16),
            pltpu.VMEM((KVH, ZH - 1, 2, ROWS, HD), BF16),
            pltpu.VMEM((KVH, QL, HD), BF16),
            pltpu.VMEM((KVH, QL, HD), BF16),
            pltpu.VMEM((KVH, 1, QL), F32),
            pltpu.VMEM((prefix + ROWS, QL), F32),
            pltpu.VMEM((2, prefix + ROWS, QL), BF16),
            pltpu.VMEM((2, prefix + ROWS, QL), BF16),
            pltpu.VMEM((RANK, 2 * ROWS), F32),
            pltpu.VMEM((RANK, 2 * ROWS), BF16),
            pltpu.VMEM((RANK, width), BF16),
            pltpu.VMEM((PIECES, RANK, PIECE // 2), BF16),
            pltpu.VMEM((PIECES, X - 1, 16, PIECE // 2), BF16),
            pltpu.VMEM((PIECES, Y - 1, 16, CHUNK), BF16),
            pltpu.VMEM((PIECES, ZH * ZL, 16, CHUNK), BF16),
            pltpu.VMEM((PIECES, RANK, PIECE // 2), BF16),
            dma((KVH, ZH - 1)), dma((KVH, ZH - 1)),
            dma((KVH, Y // 2, 2, 2)), dma((KVH, Y // 2, 2, 2)),
            dma((KVH, Y // 2, 2, 2)), dma((KVH, Y // 2, 2, 2)),
            dma((KVH, ZH - 1)), dma((KVH, ZH - 1)),
            dma((PIECES, 7, most)), dma((PIECES, 7, most)), dma((FAR,)),
        ],
        compiler_params=pltpu.CompilerParams(
            collective_id=0, has_side_effects=True, vmem_limit_bytes=56 * 1024 * 1024),
    )(
        lengths, prefix_key_rows[0], prefix_value_rows[0], response_key[0, 0], response_value[0, 0],
        prefix_middle[0], response_middle[0, 0], *far,
    )
    dkey, dvalue, resp_dkey, resp_dvalue, total = outs
    down, up, dkey, dvalue, resp_dkey, resp_dvalue = pl.pallas_call(
        results,
        out_shape=[jax.ShapeDtypeStruct((RANK, DOWN_END - DOWN), F32),
                   jax.ShapeDtypeStruct((RANK, KVH * GROUP_LANES), F32), small, small, small, small],
        in_specs=[vmem] * 5,
        out_specs=[vmem] * 6,
    )(total, dkey, dvalue, resp_dkey, resp_dvalue)
    return dkey[None], dvalue[None], resp_dkey[None, None], resp_dvalue[None, None], down.T, up


def solution(mesh):
    rows, slots = P("prompt", "resp", None), P("prompt", "resp", None, None)
    return jax.shard_map(
        local,
        mesh=mesh,
        in_specs=(rows,) * 7 + (slots,) * 7 + (P("prompt", "resp"), P()),
        out_specs=(rows, rows, slots, slots, P(), P()),
        check_vma=False,
    )
```

```python
import functools
import math

import jax
import jax.numpy as jnp
from jax import lax
from jax.experimental import pallas as pl
from jax.experimental.pallas import tpu as pltpu
from jax.sharding import PartitionSpec as P

ZL, X, C, Y, ZH = 2, 4, 2, 8, 4
HD = 128
ROWS = 64
KVH = 4
PAIR = 2
GROUPS = 5
RANK = 64
GROUP_LANES = GROUPS * HD
CHUNK = 4 * HD
PIECE = C * Y * CHUNK
PIECES = 1
FAR = 9
DOWN = KVH * GROUP_LANES
DOWN_END = DOWN + 5120
WIDTH = PIECES * PIECE
QL = 2 * ROWS * GROUPS
SCALE = HD ** -0.5
LOG2E = math.log2(math.e)
F32 = jnp.float32
BF16 = jnp.bfloat16
MESH = pl.DeviceIdType.MESH


def mod(a, n):
    return lax.rem(a + n, n)


def nt(a, b):
    return lax.dot_general(a, b, (((1,), (1,)), ((), ())), preferred_element_type=F32)


def nn(a, b):
    return lax.dot_general(a, b, (((1,), (0,)), ((), ())), preferred_element_type=F32)


def tn(a, b):
    return lax.dot_general(a, b, (((0,), (0,)), ((), ())), preferred_element_type=F32)


class Place:
    def __init__(self):
        p, r = lax.axis_index("prompt"), lax.axis_index("resp")
        self.p, self.r = p, r
        self.core = lax.rem(p, C)
        self.x = lax.rem(lax.div(p, C), X)
        self.zl = lax.div(p, C * X)
        self.y = lax.div(r, ZH)
        self.zh = lax.rem(r, ZH)
        self.z = self.zh * ZL + self.zl

    def device(self, core=None, x=None, y=None, z=None):
        core = self.core if core is None else core
        x = self.x if x is None else x
        y = self.y if y is None else y
        z = self.z if z is None else z
        zl, zh = lax.rem(z, ZL), lax.div(z, ZL)
        return {"prompt": (zl * X + x) * C + core, "resp": y * ZH + zh}


def entry_barrier(at):
    barrier = pltpu.get_barrier_semaphore()
    count = 0
    for off in range(1, C):
        pl.semaphore_signal(barrier, inc=1, device_id=at.device(core=mod(at.core + off, C)), device_id_type=MESH)
        count += 1
    for off in range(1, X):
        pl.semaphore_signal(barrier, inc=1, device_id=at.device(x=mod(at.x + off, X)), device_id_type=MESH)
        count += 1
    for off in range(1, Y):
        pl.semaphore_signal(barrier, inc=1, device_id=at.device(y=mod(at.y + off, Y)), device_id_type=MESH)
        count += 1
    for off in range(1, ZH * ZL):
        pl.semaphore_signal(barrier, inc=1, device_id=at.device(z=mod(at.z + off, ZH * ZL)), device_id_type=MESH)
        count += 1
    return lambda: pl.semaphore_wait(barrier, count)


def rcopy(src, dst, send, recv, device):
    return pltpu.make_async_remote_copy(
        src_ref=src, dst_ref=dst, send_sem=send, recv_sem=recv, device_id=device, device_id_type=MESH)


def rows_at(start, count):
    return pl.ds(pl.multiple_of(start, ROWS), count)


def when(condition, body):
    pl.when(condition)(body)


def each(n, body):
    def step(i, carry):
        body(i)
        return carry
    lax.fori_loop(0, n, step, 0)


def hops(which, way):
    return Y // 2 if which == way else Y - 1 - Y // 2


def chains(turn):
    for which in range(2):
        for way in range(2):
            turn(which, way, hops(which, way), 1 if way == 0 else -1)


class Gather:
    def __init__(self, at, kv, zs, zr, ys, yr):
        self.at, self.kv, self.zs, self.zr, self.ys, self.yr = at, kv, zs, zr, ys, yr

    def z_copy(self, h, off, sending):
        at = self.at
        zh = at.zh if sending else mod(at.zh - off, ZH)
        ref = self.kv.at[h, :, at.y, zh]
        target = at.device(z=mod(at.zh + off, ZH) * ZL + at.zl)
        return rcopy(ref, ref, self.zs.at[h, off - 1], self.zr.at[h, off - 1], target)

    def z_start(self, h):
        for off in range(1, ZH):
            self.z_copy(h, off, True).start()

    def z_wait(self, h):
        for off in range(1, ZH):
            self.z_copy(h, off, False).wait_recv()

    def y_copy(self, h, s, which, way, sign, sending):
        at = self.at
        lag = s if sending else s + 1
        ref = self.kv.at[h, which, mod(at.y - sign * lag + Y, Y)]
        return rcopy(ref, ref, self.ys.at[h, s, which, way], self.yr.at[h, s, which, way],
                     at.device(y=mod(at.y + sign, Y)))

    def y_step(self, h, s):
        def turn(which, way, count, sign):
            when((s > 0) & (s <= count), lambda: self.y_copy(h, s - 1, which, way, sign, False).wait_recv())
            when(s < count, lambda: self.y_copy(h, s, which, way, sign, True).start())
        chains(turn)

    def wait_sends(self, h):
        for off in range(1, ZH):
            self.z_copy(h, off, True).wait_send()

        def turn(which, way, count, sign):
            each(count, lambda s: self.y_copy(h, s, which, way, sign, True).wait_send())
        chains(turn)


class Scatter:
    def __init__(self, at, tm, rb, zb, ss, sr, ws, wr, outs):
        self.at, self.tm, self.rb, self.zb = at, tm, rb, zb
        self.ss, self.sr, self.ws, self.wr = ss, sr, ws, wr
        self.outs = outs

    def y_ref(self, h, s, which, count, sign):
        return self.tm.at[h, which, mod(self.at.y + sign * (count - s) + Y, Y)]

    def y_copy(self, h, s, which, way, count, sign):
        return rcopy(self.y_ref(h, s, which, count, sign), self.rb.at[h, s, which, way],
                     self.ss.at[h, s, which, way], self.sr.at[h, s, which, way],
                     self.at.device(y=mod(self.at.y + sign, Y)))

    def y_step(self, h, s):
        def turn(which, way, count, sign):
            def receive():
                self.y_copy(h, s - 1, which, way, count, sign).wait_recv()
                ref = self.y_ref(h, s, which, count, sign)
                ref[...] = (ref[...].astype(F32) + self.rb[h, s - 1, which, way].astype(F32)).astype(BF16)
            when((s > 0) & (s <= count), receive)
            when(s < count, lambda: self.y_copy(h, s, which, way, count, sign).start())
        chains(turn)

    def z_copy(self, h, off):
        at = self.at
        zh = mod(at.zh + off, ZH)
        return rcopy(self.tm.at[h, :, at.y, zh], self.zb.at[h, off - 1], self.ws.at[h, off - 1],
                     self.wr.at[h, off - 1], at.device(z=zh * ZL + at.zl))

    def z_start(self, h):
        for off in range(1, ZH):
            self.z_copy(h, off).start()

    def finish(self, h):
        at = self.at
        for off in range(1, ZH):
            self.z_copy(h, off).wait_recv()
        for which in range(2):
            total = self.tm[h, which, at.y, at.zh].astype(F32)
            for off in range(1, ZH):
                total += self.zb[h, off - 1, which].astype(F32)
            self.outs[which][:, h * HD:(h + 1) * HD] = total.astype(BF16)

    def wait_sends(self, h):
        for off in range(1, ZH):
            self.z_copy(h, off).wait_send()

        def turn(which, way, count, sign):
            each(count, lambda s: self.y_copy(h, s, which, way, count, sign).wait_send())
        chains(turn)


class Reduce:
    def __init__(self, at, src, out, rc, rx, rz, ry, part, send, recv):
        self.at, self.src, self.out = at, src, out
        self.rc, self.rx, self.rz, self.ry, self.part = rc, rx, rz, ry, part
        self.send, self.recv = send, recv
        self.n = ZH * ZL

    def rows(self, x):
        return pl.ds(pl.multiple_of(x * 16, 16), 16)

    def half(self, i, core):
        return pl.ds(pl.multiple_of(i * PIECE + core * (PIECE // 2), HD), PIECE // 2)

    def lanes(self, i, core, z):
        return pl.ds(pl.multiple_of(i * PIECE + core * (PIECE // 2) + z * CHUNK, HD), CHUNK)

    def chunk(self, z):
        return pl.ds(pl.multiple_of(z * CHUNK, HD), CHUNK)

    def sems(self, i, step, off):
        return self.send.at[i, step, off - 1], self.recv.at[i, step, off - 1]

    def core_copy(self, i):
        other = mod(self.at.core + 1, C)
        return rcopy(self.src.at[:, self.half(i, other)], self.rc.at[i], *self.sems(i, 0, 1),
                     self.at.device(core=other))

    def x_copy(self, i, off):
        x = mod(self.at.x + off, X)
        return rcopy(self.part.at[i, self.rows(x), :], self.rx.at[i, off - 1], *self.sems(i, 1, off),
                     self.at.device(x=x))

    def z_copy(self, i, off):
        z = mod(self.at.z + off, self.n)
        return rcopy(self.part.at[i, self.rows(self.at.x), self.chunk(z)], self.rz.at[i, off - 1],
                     *self.sems(i, 2, off), self.at.device(z=z))

    def y_copy(self, i, off, sending):
        y = self.at.y if sending else mod(self.at.y - off, Y)
        return rcopy(self.ry.at[i, y], self.ry.at[i, y], *self.sems(i, 3, off),
                     self.at.device(y=mod(self.at.y + off, Y)))

    def z_back(self, i, off, sending):
        z = self.at.z if sending else mod(self.at.z - off, self.n)
        ref = self.out.at[self.rows(self.at.x), self.lanes(i, self.at.core, z)]
        return rcopy(ref, ref, *self.sems(i, 4, off), self.at.device(z=mod(self.at.z + off, self.n)))

    def x_back(self, i, off, sending):
        x = self.at.x if sending else mod(self.at.x - off, X)
        ref = self.out.at[self.rows(x), self.half(i, self.at.core)]
        return rcopy(ref, ref, *self.sems(i, 5, off), self.at.device(x=mod(self.at.x + off, X)))

    def core_back(self, i, sending):
        core = self.at.core if sending else mod(self.at.core + 1, C)
        ref = self.out.at[:, self.half(i, core)]
        return rcopy(ref, ref, *self.sems(i, 6, 1), self.at.device(core=mod(self.at.core + 1, C)))

    def step(self, i, k):
        at = self.at
        if k == 0:
            self.core_copy(i).start()
        if k == 1:
            self.core_copy(i).wait_recv()
            self.part[i] = (self.src[:, self.half(i, at.core)].astype(F32) + self.rc[i].astype(F32)).astype(BF16)
            for off in range(1, X):
                self.x_copy(i, off).start()
        if k == 2:
            total = self.part[i, self.rows(at.x), :].astype(F32)
            for off in range(1, X):
                self.x_copy(i, off).wait_recv()
                total += self.rx[i, off - 1].astype(F32)
            self.part[i, self.rows(at.x), :] = total.astype(BF16)
            for off in range(1, self.n):
                self.z_copy(i, off).start()
        if k == 3:
            total = self.part[i, self.rows(at.x), self.chunk(at.z)].astype(F32)
            for off in range(1, self.n):
                self.z_copy(i, off).wait_recv()
                total += self.rz[i, off - 1].astype(F32)
            self.ry[i, at.y] = total.astype(BF16)
            for off in range(1, Y):
                self.y_copy(i, off, True).start()
        if k == 4:
            for off in range(1, Y):
                self.y_copy(i, off, False).wait_recv()
            total = self.ry[i, 0].astype(F32)
            for y in range(1, Y):
                total += self.ry[i, y].astype(F32)
            self.out[self.rows(at.x), self.lanes(i, at.core, at.z)] = total.astype(BF16)
            for off in range(1, self.n):
                self.z_back(i, off, True).start()
        if k == 5:
            for off in range(1, self.n):
                self.z_back(i, off, False).wait_recv()
            for off in range(1, X):
                self.x_back(i, off, True).start()
        if k == 6:
            for off in range(1, X):
                self.x_back(i, off, False).wait_recv()
            self.core_back(i, True).start()
        if k == 7:
            self.core_back(i, False).wait_recv()

    def wait_sends(self, i):
        self.core_copy(i).wait_send()
        self.core_back(i, True).wait_send()
        for off in range(1, X):
            self.x_copy(i, off).wait_send()
            self.x_back(i, off, True).wait_send()
        for off in range(1, self.n):
            self.z_copy(i, off).wait_send()
            self.z_back(i, off, True).wait_send()
        for off in range(1, Y):
            self.y_copy(i, off, True).wait_send()


class Attention:
    def __init__(self, at, length, refs, kv, tm, scr):
        self.at, self.length, self.kv, self.tm = at, length, kv, tm
        (self.pq, self.rq, self.pdo, self.rdo, self.po, self.ro, self.rk, self.rv, self.up_w, self.mid_t) = refs
        (self.qs, self.dos, self.delta, self.s, self.e, self.t, self.hid, self.ar_src, self.rdk, self.rdv) = scr
        self.chunk = PAIR * ZH * ROWS
        self.prefix = Y * ZH * ROWS
        lane = lax.broadcasted_iota(jnp.int32, (1, QL), 1)
        self.in_head = lax.rem(lane, 2 * ROWS)

    def keys(self, h, which, c):
        return self.kv[h, which, pl.ds(c * PAIR, PAIR)].reshape(self.chunk, HD)

    def lanes(self, h):
        return pl.ds(pl.multiple_of(h * HD, HD), HD)

    def q_lanes(self, h, i):
        return pl.ds(pl.multiple_of(h * GROUP_LANES + i * HD, HD), HD)

    def rows_of(self, c):
        return pl.ds(pl.multiple_of(c * self.chunk, self.chunk), self.chunk)

    def prepare(self, h):
        alive = lax.broadcasted_iota(jnp.int32, (ROWS, HD), 0) < self.length
        for i in range(GROUPS):
            lanes = self.q_lanes(h, i)
            top, low = pl.ds(2 * i * ROWS, ROWS), pl.ds((2 * i + 1) * ROWS, ROWS)
            self.qs[h, top, :] = self.pq[:, lanes]
            self.qs[h, low, :] = self.rq[:, lanes]
            grad_top = self.pdo[:, lanes].astype(F32)
            grad_low = jnp.where(alive, self.rdo[:, lanes].astype(F32), 0.0)
            self.dos[h, top, :] = grad_top.astype(BF16)
            self.dos[h, low, :] = grad_low.astype(BF16)
            both = jnp.concatenate(
                [grad_top * self.po[:, lanes].astype(F32), grad_low * self.ro[:, lanes].astype(F32)], axis=0)
            self.delta[h, :, i * HD:(i + 1) * HD] = jnp.sum(both.T, axis=0, keepdims=True)

    def top8(self, s, op):
        return op(s.reshape(s.shape[0] // 8, 8, QL), axis=0)

    def scores(self, h, tick):
        q = self.qs[h]
        limit = jnp.where(self.in_head < ROWS, self.at.r * ROWS + self.in_head, self.prefix)
        own_row = lax.broadcasted_iota(jnp.int32, (ROWS, QL), 0)
        row = lax.broadcasted_iota(jnp.int32, (self.chunk, QL), 0)
        s = jnp.where(own_row <= self.in_head - ROWS, nt(self.rk[:, self.lanes(h)], q), -jnp.inf)
        self.s[pl.ds(self.prefix, ROWS), :] = s

        def body(c, m8):
            tick(c)
            s = jnp.where(row + c * self.chunk <= limit, nt(self.keys(h, 0, c), q), -jnp.inf)
            self.s[self.rows_of(c), :] = s
            return jnp.maximum(m8, self.top8(s, jnp.max))

        m8 = lax.fori_loop(0, Y // PAIR, body, self.top8(s, jnp.max))
        return jnp.max(m8, axis=0, keepdims=True) * (SCALE * LOG2E)

    def weights(self, h, slot, m, tick):
        do, delta = self.dos[h], self.delta[h]

        def part(at_c, k, v):
            e = jnp.exp2(self.s[at_c, :] * (SCALE * LOG2E) - m)
            t = (e * (nt(v, do) - delta)).astype(BF16)
            self.e[slot, at_c, :] = e.astype(BF16)
            self.t[slot, at_c, :] = t
            return self.top8(e, jnp.sum), tn(k, t)

        def body(c, carry):
            tick(c)
            l8, dq = part(self.rows_of(c), self.keys(h, 0, c), self.keys(h, 1, c))
            return carry[0] + l8, carry[1] + dq

        own = part(pl.ds(self.prefix, ROWS), self.rk[:, self.lanes(h)], self.rv[:, self.lanes(h)])
        l8, dq = lax.fori_loop(0, Y // PAIR, body, own)
        inv = 1.0 / jnp.sum(l8, axis=0, keepdims=True)
        inv_col = jnp.concatenate(
            [jnp.broadcast_to(inv[:, i * HD:(i + 1) * HD], (HD, HD)).T for i in range(GROUPS)], axis=0)
        self.qs[h] = (self.qs[h].astype(F32) * (inv_col * SCALE)).astype(BF16)
        self.dos[h] = (self.dos[h].astype(F32) * inv_col).astype(BF16)
        dq_low = (dq * (inv * SCALE)).astype(BF16)
        hidden = self.hid[...]
        for i in range(GROUPS):
            piece = dq_low[:, i * HD:(i + 1) * HD]
            hidden += nn(self.up_w[:, self.q_lanes(h, i)], piece)
            lanes = self.q_lanes(h, i)
            self.ar_src[:, lanes] = nt(self.mid_t[...], piece).astype(BF16)
        self.hid[...] = hidden

    def terms(self, h, slot, tick):
        q, do = self.qs[h], self.dos[h]

        def body(c, carry):
            tick(c)
            at_c = self.rows_of(c)
            shape = (PAIR, ZH, ROWS, HD)
            self.tm[h, 0, pl.ds(c * PAIR, PAIR)] = nn(self.t[slot, at_c, :], q).astype(BF16).reshape(shape)
            self.tm[h, 1, pl.ds(c * PAIR, PAIR)] = nn(self.e[slot, at_c, :], do).astype(BF16).reshape(shape)
            return carry

        lax.fori_loop(0, Y // PAIR, body, 0)
        own = pl.ds(self.prefix, ROWS)
        self.rdk[:, self.lanes(h)] = nn(self.t[slot, own, :], q).astype(BF16)
        self.rdv[:, self.lanes(h)] = nn(self.e[slot, own, :], do).astype(BF16)


def down_terms(hid, px, rx, ar_src):
    hidden = hid[...].astype(BF16)
    for j in range(0, DOWN_END - DOWN, 512):
        lanes = slice(j, j + 512)
        ar_src[:, DOWN + j:DOWN + j + 512] = (
            nn(hidden[:, :ROWS], px[:, lanes]) + nn(hidden[:, ROWS:], rx[:, lanes])).astype(BF16)


def kernel(length_ref, pk, pv, rk, rv, pm, rm, *rest):
    far, rest = rest[:FAR], rest[FAR:]
    (pdk, pdv, rdk, rdv, total), rest = rest[:5], rest[5:]
    near, rest = rest[:FAR], rest[FAR:]
    (kv, tm, rb, zb, qs, dos, delta, s_scr, e_scr, t_scr, hid, mid_t, ar_src, rc, rx_b, ry, rz, part,
     gzs, gzr, gys, gyr, sys, syr, szs, szr, asend, arecv, loaded) = rest
    pq, rq, pdo, rdo, po, ro, up_w, px, rx = near
    at = Place()
    gather = Gather(at, kv, gzs, gzr, gys, gyr)
    scatter = Scatter(at, tm, rb, zb, sys, syr, szs, szr, (pdk, pdv))
    reduce = Reduce(at, ar_src, total, rc, rx_b, ry, rz, part, asend, arecv)
    refs = (pq, rq, pdo, rdo, po, ro, rk, rv, up_w, mid_t)
    scr = (qs, dos, delta, s_scr, e_scr, t_scr, hid, ar_src, rdk, rdv)
    attention = Attention(at, length_ref[0, 0], refs, kv, tm, scr)
    parts = Y // PAIR
    last = Y // 2

    everyone_in = entry_barrier(at)
    loads = [pltpu.make_async_copy(far[i], near[i], loaded.at[i]) for i in range(FAR)]
    for load in loads:
        load.start()
    for h in range(KVH):
        kv[h, 0, at.y, at.zh] = pk[:, h * HD:(h + 1) * HD]
        kv[h, 1, at.y, at.zh] = pv[:, h * HD:(h + 1) * HD]
    everyone_in()
    each(KVH, gather.z_start)
    hid[...] = jnp.zeros_like(hid)
    ar_src[:, DOWN_END:] = jnp.zeros((RANK, WIDTH - DOWN_END), BF16)
    mid_t[...] = jnp.concatenate([pm[...].astype(F32).T, rm[...].astype(F32).T], axis=1).astype(BF16)

    for load in loads:
        load.wait()

    def begin(h):
        gather.z_wait(h)
        gather.y_step(h, 0)
    each(2, begin)

    def first(s):
        attention.prepare(s)
        each(2, lambda h: gather.y_step(h, s + 1))
    each(last - 1, first)
    each(2, lambda i: begin(i + 2))
    first(last - 1)

    def second(h):
        def tick(unit):
            def at_part(c):
                slot = (h * 3 + unit) * parts + c

                when((slot < 18) & (lax.rem(slot, 7) == 2), lambda: gather.y_step(2, lax.div(slot, 7) + 1))
                when(slot == 5, lambda: gather.y_step(3, 1))
                when(slot == 14, lambda: gather.y_step(3, 2))
            return at_part
        m = attention.scores(h, tick(0))
        attention.weights(h, h, m, tick(1))
        attention.terms(h, h, tick(2))
    each(2, second)

    gather.y_step(2, last)
    gather.y_step(3, last - 1)
    scatter.y_step(0, 0)
    m = attention.scores(2, lambda c: None)
    scatter.y_step(1, 0)
    attention.weights(2, 0, m, lambda c: None)
    gather.y_step(3, last)

    scatter.y_step(0, 1)
    m = attention.scores(3, lambda c: None)
    scatter.y_step(1, 1)
    scatter.y_step(0, 2)
    attention.weights(3, 1, m, lambda c: None)

    def sums(k):
        each(PIECES, lambda i: reduce.step(i, k))

    down_terms(hid, px, rx, ar_src)
    sums(0)
    attention.terms(2, 0, lambda c: None)
    scatter.y_step(0, 3)
    scatter.y_step(1, 2)
    scatter.y_step(2, 0)
    sums(1)
    attention.terms(3, 1, lambda c: None)
    scatter.y_step(3, 0)
    scatter.y_step(0, 4)
    scatter.z_start(0)
    sums(2)
    scatter.y_step(1, 3)
    scatter.y_step(2, 1)
    sums(3)
    scatter.y_step(3, 1)
    scatter.y_step(1, 4)
    scatter.z_start(1)
    sums(4)
    scatter.y_step(2, 2)
    scatter.y_step(3, 2)
    sums(5)
    scatter.y_step(2, 3)
    scatter.y_step(3, 3)
    sums(6)
    scatter.y_step(2, 4)
    scatter.z_start(2)
    scatter.y_step(3, 4)
    scatter.z_start(3)
    sums(7)
    for h in range(KVH):
        scatter.finish(h)
    each(KVH, gather.wait_sends)
    each(KVH, scatter.wait_sends)
    each(PIECES, reduce.wait_sends)


def results(total, pdk, pdv, rdk, rdv, down, up, *low):
    for src, dst in zip((pdk, pdv, rdk, rdv), low):
        dst[...] = src[...]
    down[...] = 2.0 * total[:, DOWN:DOWN_END].astype(F32)
    up[...] = 2.0 * total[:, :DOWN].astype(F32)


def local(
    prefix_input, prefix_query_rows, prefix_key_rows, prefix_value_rows, prefix_output, prefix_output_grad,
    prefix_middle, response_input, response_query, response_key, response_value, response_output,
    response_output_grad, response_middle, lengths, adapter_up_weight,
):
    prefix = Y * ZH * ROWS
    width = WIDTH
    vmem = pl.BlockSpec(memory_space=pltpu.VMEM)
    kv_width = KVH * HD
    dma = pltpu.SemaphoreType.DMA
    most = max(Y, ZH * ZL, X) - 1
    small = jax.ShapeDtypeStruct((ROWS, kv_width), BF16)
    far = (prefix_query_rows[0], response_query[0, 0], prefix_output_grad[0], response_output_grad[0, 0],
           prefix_output[0], response_output[0, 0], adapter_up_weight, prefix_input[0], response_input[0, 0])
    outs = pl.pallas_call(
        kernel,
        out_shape=[small, small, small, small, jax.ShapeDtypeStruct((RANK, width), BF16)],
        in_specs=[pl.BlockSpec(memory_space=pltpu.SMEM)] + [vmem] * 6 + [pl.BlockSpec(memory_space=pl.ANY)] * FAR,
        out_specs=[vmem] * 5,
        scratch_shapes=[pltpu.VMEM(a.shape, BF16) for a in far] + [
            pltpu.VMEM((KVH, 2, Y, ZH, ROWS, HD), BF16),
            pltpu.VMEM((KVH, 2, Y, ZH, ROWS, HD), BF16),
            pltpu.VMEM((KVH, Y // 2, 2, 2, ZH, ROWS, HD), BF16),
            pltpu.VMEM((KVH, ZH - 1, 2, ROWS, HD), BF16),
            pltpu.VMEM((KVH, QL, HD), BF16),
            pltpu.VMEM((KVH, QL, HD), BF16),
            pltpu.VMEM((KVH, 1, QL), F32),
            pltpu.VMEM((prefix + ROWS, QL), F32),
            pltpu.VMEM((2, prefix + ROWS, QL), BF16),
            pltpu.VMEM((2, prefix + ROWS, QL), BF16),
            pltpu.VMEM((RANK, 2 * ROWS), F32),
            pltpu.VMEM((RANK, 2 * ROWS), BF16),
            pltpu.VMEM((RANK, width), BF16),
            pltpu.VMEM((PIECES, RANK, PIECE // 2), BF16),
            pltpu.VMEM((PIECES, X - 1, 16, PIECE // 2), BF16),
            pltpu.VMEM((PIECES, Y - 1, 16, CHUNK), BF16),
            pltpu.VMEM((PIECES, ZH * ZL, 16, CHUNK), BF16),
            pltpu.VMEM((PIECES, RANK, PIECE // 2), BF16),
            dma((KVH, ZH - 1)), dma((KVH, ZH - 1)),
            dma((KVH, Y // 2, 2, 2)), dma((KVH, Y // 2, 2, 2)),
            dma((KVH, Y // 2, 2, 2)), dma((KVH, Y // 2, 2, 2)),
            dma((KVH, ZH - 1)), dma((KVH, ZH - 1)),
            dma((PIECES, 7, most)), dma((PIECES, 7, most)), dma((FAR,)),
        ],
        compiler_params=pltpu.CompilerParams(
            collective_id=0, has_side_effects=True, vmem_limit_bytes=56 * 1024 * 1024),
    )(
        lengths, prefix_key_rows[0], prefix_value_rows[0], response_key[0, 0], response_value[0, 0],
        prefix_middle[0], response_middle[0, 0], *far,
    )
    dkey, dvalue, resp_dkey, resp_dvalue, total = outs
    down, up, dkey, dvalue, resp_dkey, resp_dvalue = pl.pallas_call(
        results,
        out_shape=[jax.ShapeDtypeStruct((RANK, DOWN_END - DOWN), F32),
                   jax.ShapeDtypeStruct((RANK, KVH * GROUP_LANES), F32), small, small, small, small],
        in_specs=[vmem] * 5,
        out_specs=[vmem] * 6,
    )(total, dkey, dvalue, resp_dkey, resp_dvalue)
    return dkey[None], dvalue[None], resp_dkey[None, None], resp_dvalue[None, None], down.T, up


def solution(mesh):
    rows, slots = P("prompt", "resp", None), P("prompt", "resp", None, None)
    return jax.shard_map(
        local,
        mesh=mesh,
        in_specs=(rows,) * 7 + (slots,) * 7 + (P("prompt", "resp"), P()),
        out_specs=(rows, rows, slots, slots, P(), P()),
        check_vma=False,
    )
```
